256 devices in a mesh: seq: 64 (over y, z, core), tp: 4 (over x).
Axes of the slice: x: 4, y: 4, z: 8, core: 2. Of those that a mesh axis runs over, the one named last changes fastest.
Arguments:
- tokens: int32 [8192], P('seq'), may hold values from 0 to 511
- table: bfloat16 [512, 3, 4096], P(None, None, 'tp'), may hold values from -6 to 6
- short_kernel: float32 [3, 3, 4096], P(None, None, 'tp'), may hold values from -4 to 4
- poles: float32 [16, 4096], P(None, 'tp'), may hold values from 0 to 1, as said below
- residues: float32 [16, 4096], P(None, 'tp'), may hold values from -1 to 1
- skip: float32 [4096], P('tp'), may hold values from -4 to 4
- out_weight: bfloat16 [4096, 4096], P(('tp', 'seq')), may hold values from -0.09375 to 0.09375
Outputs:
- mixed_out: bfloat16 [8192, 4096], P(('seq', 'tp'))
The draws below stay inside these ranges and needn't reach their ends.
Inputs may be any that keep to these rules, and one draw needn't show every extreme that they name: poles lie strictly between 0 and 1.
All inputs are finite; a program needn't handle non-finite values.
Results may differ from the reference program's by a relative error of at most 0.0121.
Values may be sent and summed in bfloat16 or wider, within the bound.
No kernel may reach another device: no remote copies, remote signals or barrier semaphores. Data moves between devices by JAX's collectives and lax.ppermute only.
A program may use at most 192 MiB of HBM per device.

```python
import math
import jax
import jax.numpy as jnp
import numpy as np
from jax import lax

D = 4096
VOCAB = 512
ORDER = 16
TOK_DEV = 128
BLOCK = 64
TOKENS = 8192
N_TP = 4


def modal_rates(key, slow_share, middle_share):
    first, second, third, fourth = jax.random.split(key, 4)
    choose = jax.random.uniform(first, (ORDER, D))
    slow_rate = jnp.exp(jax.random.uniform(second, (ORDER, D), minval=math.log(0.1), maxval=math.log(2.0))) / TOKENS
    middle_rate = jnp.exp(jax.random.uniform(fourth, (ORDER, D), minval=math.log(2.3), maxval=math.log(2.0 * TOKENS / TOK_DEV))) / TOKENS
    fast_rate = jnp.exp(jax.random.uniform(third, (ORDER, D), minval=math.log(1.0 / 48.0), maxval=math.log(1.0 / 6.0)))
    return jnp.where(choose < slow_share, slow_rate, jnp.where(choose < slow_share + middle_share, middle_rate, fast_rate))


def draw_poles(key, part):
    slow_share = 0.4
    return jnp.exp(-modal_rates(key, slow_share, 0.35)).astype(jnp.float32)


def draw_residues(key, part):
    slow_share = 0.4
    pole_values = jnp.exp(-modal_rates(key, slow_share, 0.35))
    key = jax.random.fold_in(key, 7)
    signs = jnp.clip(jax.random.normal(key, (ORDER, D)), -4.0, 4.0)
    return (0.25 * signs * jnp.sqrt(1.0 - pole_values * pole_values)).astype(jnp.float32)


def set_ends(array, key, smallest, top_value):
    longest = array.shape.index(max(array.shape))
    spots = []
    for shift in (0, 1):
        where = [jax.random.randint(jax.random.fold_in(key, axis), (), 0, length) for axis, length in enumerate(array.shape)]
        where[longest] = (where[longest] + shift) % array.shape[longest]
        spots.append(tuple(where))
    return array.at[spots[0]].set(smallest).at[spots[1]].set(top_value)


def level_of(own_key, shape, pieces, smallest, top_value):
    gain, own = 1.0, jax.random.fold_in(own_key, 6)
    for axis_at, parts in pieces:
        draws = jnp.exp(jax.random.uniform(jax.random.fold_in(own, axis_at), (parts,), jnp.float32, smallest / len(pieces), top_value / len(pieces)))
        gain = gain * jnp.repeat(draws, shape[axis_at] // parts).reshape([-1 if axis == axis_at else 1 for axis in range(len(shape))])
    return gain


def cumulative_ranks(amount, slope):
    loads = [(1 << 20) // math.isqrt(grade ** slope) + 1 for grade in range(1, amount + 1)]
    spread = 1 + sum(loads) // (1 << 30)
    return np.cumsum(np.array([max(1, weight // spread) for weight in loads]))


def ranked_ids(rng, extent, number_of, lean):
    grid = cumulative_ranks(number_of, lean)
    ticket = jax.random.randint(jax.random.fold_in(rng, 1), extent, 0, int(grid[number_of - 1]))
    rank = jnp.searchsorted(jnp.asarray(grid, jnp.int32), ticket, side="right")
    return jax.random.permutation(jax.random.fold_in(rng, 2), number_of)[rank].astype(jnp.int32)


def centred(own_key, extent, scale, bound, cuts=(), dtype=jnp.bfloat16):
    values = scale * jax.random.normal(own_key, extent, jnp.float32)
    if cuts:
        values = values * level_of(own_key, extent, cuts, -0.22, 0.18)
    return jnp.clip(values, -bound, bound).astype(dtype)


def setup_inputs(seed: int = 0) -> dict:
    key_of = jax.random.split(jax.random.key(seed), 8)
    tokens = set_ends(ranked_ids(key_of[0], (TOKENS,), VOCAB, 2), jax.random.fold_in(key_of[0], 3), 0, VOCAB - 1).astype(jnp.int32)
    table = centred(key_of[1], (VOCAB, 3, D), 1.0, 6.0, ((2, 4),))
    short_kernel = centred(key_of[2], (3, 3, D), 0.6, 4.0, ((2, 4),), jnp.float32)
    poles = draw_poles(jax.random.fold_in(key_of[7], 71), 0)
    residues = draw_residues(jax.random.fold_in(key_of[7], 71), 0)
    skip = centred(key_of[5], (D,), 1.0, 4.0, ((0, 4),), jnp.float32)
    out_weight = centred(key_of[6], (D, D), D ** -0.5, 0.09375, ((0, 256),))
    return {"tokens": tokens, "table": table, "short_kernel": short_kernel, "poles": poles, "residues": residues, "skip": skip, "out_weight": out_weight}


def reference(tokens, table, short_kernel, poles, residues, skip, out_weight):
    width = table.shape[2]
    group = width // N_TP
    token_blocks = tokens.reshape(-1, BLOCK)

    def convolve_block(carry, ids):
        state, before = carry
        current = table[ids].astype(jnp.float32)
        extended = jnp.concatenate([before, current], axis=0)
        mixed = short_kernel[0] * extended[2:] + short_kernel[1] * extended[1:-1] + short_kernel[2] * extended[:-2]
        query = mixed[:, 0]
        drive = mixed[:, 1] * mixed[:, 2]

        def advance(modes, value):
            modes = poles * modes + value[None, :]
            return modes, jnp.sum(residues * modes, axis=0)

        state, filtered = lax.scan(advance, state, drive)
        gated = (query * (filtered + skip * drive)).astype(jnp.bfloat16)
        total = jnp.zeros((ids.shape[0], width), jnp.float32)
        for index in range(N_TP):
            part = jnp.dot(gated[:, index * group:(index + 1) * group], out_weight[index * group:(index + 1) * group], preferred_element_type=jnp.float32).astype(jnp.bfloat16)
            total = total + lax.optimization_barrier(part).astype(jnp.float32)
        return (state, current[BLOCK - 2:]), total.astype(jnp.bfloat16)

    start = (jnp.zeros((ORDER, width), jnp.float32), jnp.zeros((2, 3, width), jnp.float32))
    _, result = lax.scan(convolve_block, start, token_blocks)
    return result.reshape(-1, width)
```

```python
import functools

import jax
import jax.numpy as jnp
from jax import lax
from jax.experimental import pallas as pl
from jax.experimental.pallas import tpu as pltpu
from jax.sharding import PartitionSpec as P

F32 = jnp.float32
BF16 = jnp.bfloat16
TOK = 128
HALF = 512
MODES = 16
STEP = 136
VMEM = 48 * 1024 * 1024


def segment_rows(t):
    return pl.ds(t, 8, stride=STEP)


def spread(scratch, value, first):
    for q in range(4):
        scratch[pl.ds(first + q, MODES, stride=8), :] = value[:, q * 128 : (q + 1) * 128]


def squared(value, times):
    for _ in range(times):
        value = value * value
    return value


def scan_kernel(
    info, own, other, before_a, before_b, table, taps, poles, residues, skip,
    query_out, base_out, states_out, first_out,
    streams, drive_scr, filt_scr, pole_scr, res_scr, state_scr,
):
    core, chip = info[0], info[1]
    ids_own, ids_other = own[...], other[...]
    first = jnp.where(core == 0, ids_own, ids_other)
    second = jnp.where(core == 0, ids_other, ids_own)
    before = jnp.where(chip == 0, -1, before_a[...] + before_b[...])
    hots = []
    for ids, low in ((before, TOK - 16), (first, 0), (second, 0)):
        column = jnp.transpose(jnp.broadcast_to(ids, (128, TOK)))[low:]
        parts = [
            (column == lax.broadcasted_iota(jnp.int32, column.shape, 1) + 128 * k).astype(F32)
            for k in range(4)
        ]
        hots.append(jnp.concatenate(parts, axis=1))
    hot = jnp.concatenate(hots, axis=0).astype(BF16)
    for j in range(3):
        streams[j] = jnp.dot(hot, table[j], preferred_element_type=F32)

    def mixed(j):
        return (
            taps[0, j : j + 1] * streams[j, 16 : 16 + 2 * TOK]
            + taps[1, j : j + 1] * streams[j, 15 : 15 + 2 * TOK]
            + taps[2, j : j + 1] * streams[j, 14 : 14 + 2 * TOK]
        )

    drive = mixed(1) * mixed(2)
    for s in range(2):
        for q in range(4):
            row = (s * 4 + q) * STEP
            drive_scr[row : row + TOK] = drive[s * TOK : (s + 1) * TOK, q * 128 : (q + 1) * 128]
    for first_row in (0, 4):
        spread(pole_scr, poles[...], first_row)
        spread(res_scr, residues[...], first_row)
    pole = [pole_scr[n * 8 : (n + 1) * 8] for n in range(MODES)]
    res = [res_scr[n * 8 : (n + 1) * 8] for n in range(MODES)]

    def advance(t, modes):
        value = drive_scr[segment_rows(t), :]
        modes = tuple(pole[n] * modes[n] + value for n in range(MODES))
        terms = [res[n] * modes[n] for n in range(MODES)]
        while len(terms) > 1:
            terms = [a + b for a, b in zip(terms[::2], terms[1::2])]
        filt_scr[segment_rows(t), :] = terms[0]
        return modes

    modes = lax.fori_loop(0, TOK, advance, (jnp.zeros((8, 128), F32),) * MODES, unroll=4)
    for n in range(MODES):
        state_scr[n * 8 : (n + 1) * 8] = modes[n]
    query = mixed(0)
    query_out[...] = query
    ends = []
    for q in range(4):
        lanes = slice(q * 128, (q + 1) * 128)
        one = state_scr[pl.ds(q, MODES, stride=8), :]
        two = state_scr[pl.ds(4 + q, MODES, stride=8), :]
        first_out[q * MODES : (q + 1) * MODES] = one
        ends.append((squared(poles[:, lanes], 7) * one + two).astype(BF16))
        for s in range(2):
            rows = slice(s * TOK, (s + 1) * TOK)
            row = (s * 4 + q) * STEP
            filtered = filt_scr[row : row + TOK] + skip[:, lanes] * drive[rows, lanes]
            base_out[rows, lanes] = query[rows, lanes] * filtered
    end = jnp.concatenate(ends, axis=0)
    for chip_to in range(states_out.shape[0]):
        states_out[chip_to] = end


def gate_kernel(
    info, states, first, poles, residues, query, base, keep_out, send_out, coef_scr, pole_scr, corr_scr, gated_scr
):
    core, chip, place, groups = info[0], info[1], info[2], keep_out.shape[0] // 32
    flat = [poles[:, q * 128 : (q + 1) * 128] for q in range(4)]
    pole = jnp.concatenate(flat, axis=0)
    lead = jnp.concatenate([residues[:, q * 128 : (q + 1) * 128] for q in range(4)], axis=0) * pole
    half = squared(pole, 7)
    whole = half * half

    def join(source, running):
        return whole * running + states[source].astype(F32)

    incoming = lax.fori_loop(0, chip, join, jnp.zeros((4 * MODES, 128), F32))
    coefs = (lead * incoming, lead * (half * incoming + first[...]))
    for s in range(2):
        for q in range(4):
            coef_scr[pl.ds(s * 4 + q, MODES, stride=8), :] = coefs[s][q * MODES : (q + 1) * MODES]
        spread(pole_scr, poles[...], s * 4)
    mode_pole = [pole_scr[n * 8 : (n + 1) * 8] for n in range(MODES)]
    start = tuple(coef_scr[n * 8 : (n + 1) * 8] for n in range(MODES))

    def decay(t, terms):
        total = list(terms)
        while len(total) > 1:
            total = [a + b for a, b in zip(total[::2], total[1::2])]
        corr_scr[segment_rows(t), :] = total[0]
        return tuple(mode_pole[n] * terms[n] for n in range(MODES))

    lax.fori_loop(0, TOK, decay, start, unroll=4)
    for s in range(2):
        for q in range(4):
            rows, lanes = slice(s * TOK, (s + 1) * TOK), slice(q * 128, (q + 1) * 128)
            row = (s * 4 + q) * STEP
            gated_scr[rows, lanes] = base[rows, lanes] + query[rows, lanes] * corr_scr[row : row + TOK]
    for d in range(groups):
        spot = lax.rem(place + d, groups) * 32
        for out, whose in ((keep_out, core), (send_out, 1 - core)):
            rows = pl.ds(pl.multiple_of(whose * TOK + spot, 32), 32)
            out[d * 32 : (d + 1) * 32] = gated_scr[rows, :].astype(BF16)


def project_kernel(info, keep, came, weight, *outs):
    core = info[0]
    mine = weight[pl.ds(pl.multiple_of(core * HALF, HALF), HALF), :]
    theirs = weight[pl.ds(pl.multiple_of((1 - core) * HALF, HALF), HALF), :]
    total = jnp.dot(keep[...], mine, preferred_element_type=F32) + jnp.dot(
        came[...], theirs, preferred_element_type=F32
    )
    for d, out in enumerate(outs):
        out[...] = total[d * 32 : (d + 1) * 32].astype(BF16)


def whole_block(shape):
    return pl.BlockSpec(shape, lambda i, info: (0,) * len(shape))


def core_block(shape):
    return pl.BlockSpec(shape, lambda i, info: (0,) * (len(shape) - 1) + (info[0],))


def call(kernel, name, info, args, in_specs, out_shape, out_specs, scratch=(), grid=1, flops=0, moved=0):
    return pl.pallas_call(
        kernel,
        grid_spec=pltpu.PrefetchScalarGridSpec(
            num_scalar_prefetch=1, grid=(grid,), in_specs=in_specs, out_specs=out_specs, scratch_shapes=scratch
        ),
        out_shape=out_shape,
        compiler_params=pltpu.CompilerParams(vmem_limit_bytes=VMEM),
        cost_estimate=pl.CostEstimate(flops=flops, bytes_accessed=moved, transcendentals=0),
        name=name,
    )(info, *args)


def body(tokens, table, short_kernel, poles, residues, skip, out_weight):
    n_seq, n_tp = lax.axis_size("seq"), lax.axis_size("tp")
    chips = n_seq // 2
    vocab, width = table.shape[0], out_weight.shape[1]
    index = lax.axis_index("seq")
    info = jnp.stack([index % 2, index // 2, lax.axis_index("tp")]).astype(jnp.int32)
    swap = [(i, i ^ 1) for i in range(n_seq)]
    weight = lax.all_gather(out_weight, "seq", axis=0, tiled=True)

    ids = tokens.reshape(1, TOK)
    other = lax.ppermute(ids, "seq", swap)
    before_a = lax.ppermute(ids, "seq", [(2 * p + 1, 2 * p + 2) for p in range(chips - 1)])
    before_b = lax.ppermute(ids, "seq", [(2 * p + 1, 2 * p + 3) for p in range(chips - 1)])
    ids_block = whole_block((1, TOK))
    tok_block = whole_block((2 * TOK, HALF))
    query, base, states, first = call(
        scan_kernel, "scan", info,
        (ids, other, before_a, before_b, jnp.transpose(table, (1, 0, 2)), short_kernel, poles, residues, skip.reshape(1, -1)),
        [ids_block] * 4
        + [core_block((3, vocab, HALF)), core_block((3, 3, HALF)), core_block((MODES, HALF)), core_block((MODES, HALF)), core_block((1, HALF))],
        (
            jax.ShapeDtypeStruct((2 * TOK, HALF), F32),
            jax.ShapeDtypeStruct((2 * TOK, HALF), F32),
            jax.ShapeDtypeStruct((chips, 4 * MODES, 128), BF16),
            jax.ShapeDtypeStruct((4 * MODES, 128), F32),
        ),
        (tok_block, tok_block, whole_block((chips, 4 * MODES, 128)), whole_block((4 * MODES, 128))),
        scratch=(
            pltpu.VMEM((3, 2 * TOK + 16, HALF), F32),
            pltpu.VMEM((8 * STEP, 128), F32),
            pltpu.VMEM((8 * STEP, 128), F32),
            pltpu.VMEM((MODES * 8, 128), F32),
            pltpu.VMEM((MODES * 8, 128), F32),
            pltpu.VMEM((MODES * 8, 128), F32),
        ),
        flops=600_000_000, moved=4_000_000,
    )
    states = lax.all_to_all(
        states, "seq", 0, 0, axis_index_groups=[[2 * p + c for p in range(chips)] for c in range(2)]
    )
    keep, send = call(
        gate_kernel, "gate", info, (states, first, poles, residues, query, base),
        [whole_block((chips, 4 * MODES, 128)), whole_block((4 * MODES, 128)), core_block((MODES, HALF)), core_block((MODES, HALF)), tok_block, tok_block],
        (jax.ShapeDtypeStruct((TOK, HALF), BF16),) * 2,
        (whole_block((TOK, HALF)),) * 2,
        scratch=(
            pltpu.VMEM((MODES * 8, 128), F32),
            pltpu.VMEM((MODES * 8, 128), F32),
            pltpu.VMEM((8 * STEP, 128), F32),
            pltpu.VMEM((2 * TOK, HALF), F32),
        ),
        flops=20_000_000, moved=2_000_000,
    )
    came = lax.ppermute(send, "seq", swap)
    tile = 512
    rows = TOK // n_tp
    parts = call(
        project_kernel, "project", info, (keep, came, weight),
        [whole_block((TOK, HALF)), whole_block((TOK, HALF)), pl.BlockSpec((2 * HALF, tile), lambda i, info: (0, i))],
        (jax.ShapeDtypeStruct((rows, width), BF16),) * n_tp,
        (pl.BlockSpec((rows, tile), lambda i, info: (0, i)),) * n_tp,
        grid=width // tile, flops=2 * TOK * 2 * HALF * width, moved=2 * HALF * width * 2,
    )
    total = parts[0].astype(F32)
    for d in range(1, n_tp):
        total = total + lax.ppermute(parts[d], "tp", [(x, (x + d) % n_tp) for x in range(n_tp)]).astype(F32)
    return total.astype(BF16)


def solution(mesh):
    placed = (
        P("seq"),
        P(None, None, "tp"),
        P(None, None, "tp"),
        P(None, "tp"),
        P(None, "tp"),
        P("tp"),
        P(("tp", "seq"), None),
    )
    return jax.shard_map(
        body, mesh=mesh, in_specs=placed, out_specs=P(("seq", "tp"), None), check_vma=False
    )
```

```python
import functools

import jax
import jax.numpy as jnp
from jax import lax
from jax.experimental import pallas as pl
from jax.experimental.pallas import tpu as pltpu
from jax.sharding import PartitionSpec as P

F32 = jnp.float32
BF16 = jnp.bfloat16
TOK = 128
HALF = 512
MODES = 16
STEP = 136
VMEM = 62 * 1024 * 1024
NZ = 8
ALONG = (0, -1, 1, -2, 2, -3, 3)


def segment_rows(t):
    return pl.ds(t, 8, stride=STEP)


def spread(scratch, value, first):
    for q in range(4):
        scratch[pl.ds(first + q, MODES, stride=8), :] = value[:, q * 128 : (q + 1) * 128]


def squared(value, times):
    for _ in range(times):
        value = value * value
    return value


def scan_kernel(
    info, own, other, passed, table, taps, poles, residues, skip,
    query_out, base_out, states_out, first_out,
    streams, drive_scr, filt_scr, pole_scr, res_scr, state_scr,
):
    core, chip = info[0], info[1]
    ids_own, ids_other = own[...], other[0:1]
    first = jnp.where(core == 0, ids_own, ids_other)
    second = jnp.where(core == 0, ids_other, ids_own)
    before = jnp.where(chip == 0, -1, jnp.where(core == 0, passed[...], other[1:2]))
    hots = []
    for ids, low in ((before, TOK - 16), (first, 0), (second, 0)):
        column = jnp.transpose(jnp.broadcast_to(ids, (128, TOK)))[low:]
        parts = [
            (column == lax.broadcasted_iota(jnp.int32, column.shape, 1) + 128 * k).astype(F32)
            for k in range(4)
        ]
        hots.append(jnp.concatenate(parts, axis=1))
    hot = jnp.concatenate(hots, axis=0).astype(BF16)
    for j in range(3):
        streams[j] = jnp.dot(hot, table[j], preferred_element_type=F32)

    def mixed(j):
        return (
            taps[0, j : j + 1] * streams[j, 16 : 16 + 2 * TOK]
            + taps[1, j : j + 1] * streams[j, 15 : 15 + 2 * TOK]
            + taps[2, j : j + 1] * streams[j, 14 : 14 + 2 * TOK]
        )

    drive = mixed(1) * mixed(2)
    for s in range(2):
        for q in range(4):
            row = (s * 4 + q) * STEP
            drive_scr[row : row + TOK] = drive[s * TOK : (s + 1) * TOK, q * 128 : (q + 1) * 128]
    for first_row in (0, 4):
        spread(pole_scr, poles[...], first_row)
        spread(res_scr, residues[...], first_row)
    pole = [pole_scr[n * 8 : (n + 1) * 8] for n in range(MODES)]
    res = [res_scr[n * 8 : (n + 1) * 8] for n in range(MODES)]

    def advance(t, modes):
        value = drive_scr[segment_rows(t), :]
        modes = tuple(pole[n] * modes[n] + value for n in range(MODES))
        terms = [res[n] * modes[n] for n in range(MODES)]
        while len(terms) > 1:
            terms = [a + b for a, b in zip(terms[::2], terms[1::2])]
        filt_scr[segment_rows(t), :] = terms[0]
        return modes

    modes = lax.fori_loop(0, TOK, advance, (jnp.zeros((8, 128), F32),) * MODES, unroll=4)
    for n in range(MODES):
        state_scr[n * 8 : (n + 1) * 8] = modes[n]
    query = mixed(0)
    query_out[...] = query
    ends = []
    for q in range(4):
        lanes = slice(q * 128, (q + 1) * 128)
        rows = slice(q * MODES, (q + 1) * MODES)
        one = state_scr[pl.ds(q, MODES, stride=8), :]
        two = state_scr[pl.ds(4 + q, MODES, stride=8), :]
        half = squared(poles[:, lanes], 7)
        first_out[rows] = one
        ends.append((half * one + two).astype(BF16))
        for s in range(2):
            rows = slice(s * TOK, (s + 1) * TOK)
            row = (s * 4 + q) * STEP
            filtered = filt_scr[row : row + TOK] + skip[:, lanes] * drive[rows, lanes]
            base_out[rows, lanes] = query[rows, lanes] * filtered
    end = jnp.concatenate(ends, axis=0)
    for chip_to in range(states_out.shape[0]):
        states_out[chip_to] = end


def gate_kernel(
    groups, info, states, first, poles, residues, query, base, gated_out, coef_scr, pole_scr, corr_scr, gated_scr
):
    place, each = info[2], TOK // groups
    pole = jnp.concatenate([poles[:, q * 128 : (q + 1) * 128] for q in range(4)], axis=0)
    lead = jnp.concatenate([residues[:, q * 128 : (q + 1) * 128] for q in range(4)], axis=0) * pole
    half = squared(pole, 7)
    whole = half * half

    def join(source, running):
        return whole * running + states[source].astype(F32)

    incoming = lax.fori_loop(0, info[1], join, jnp.zeros((4 * MODES, 128), F32))
    coefs = (lead * incoming, lead * (half * incoming + first[...]))
    for s in range(2):
        for q in range(4):
            coef_scr[pl.ds(s * 4 + q, MODES, stride=8), :] = coefs[s][q * MODES : (q + 1) * MODES]
        spread(pole_scr, poles[...], s * 4)
    mode_pole = [pole_scr[n * 8 : (n + 1) * 8] for n in range(MODES)]
    start = tuple(coef_scr[n * 8 : (n + 1) * 8] for n in range(MODES))

    def decay(t, terms):
        total = list(terms)
        while len(total) > 1:
            total = [a + b for a, b in zip(total[::2], total[1::2])]
        corr_scr[segment_rows(t), :] = total[0]
        return tuple(mode_pole[n] * terms[n] for n in range(MODES))

    lax.fori_loop(0, TOK, decay, start, unroll=4)
    for s in range(2):
        for q in range(4):
            rows, lanes = slice(s * TOK, (s + 1) * TOK), slice(q * 128, (q + 1) * 128)
            row = (s * 4 + q) * STEP
            gated_scr[rows, lanes] = base[rows, lanes] + query[rows, lanes] * corr_scr[row : row + TOK]
    for owner in range(2):
        for d in range(groups):
            spot = pl.ds(pl.multiple_of(owner * TOK + lax.rem(place + d, groups) * each, each), each)
            row = owner * TOK + d * each
            gated_out[row : row + each] = gated_scr[spot, :].astype(BF16)


def place_kernel(info, *refs):
    column, blocks, last, outs = info[4], refs[:7], refs[7:9], refs[9:]
    for block, dz in zip(blocks, ALONG):
        rows = pl.ds(pl.multiple_of(lax.rem(column + dz + NZ, NZ) * 32, 32), 32)
        for k, out in enumerate(outs):
            cols = out.shape[1]
            out[rows, :] = block[:, k * cols : (k + 1) * cols]
    rows = pl.ds(pl.multiple_of(lax.rem(column + NZ // 2, NZ) * 32, 32), 32)
    for block, out in zip(last, outs):
        out[rows, :] = block[...]


def project_kernel(rows_of, info, ours, theirs, *refs):
    core, row = info[0], info[3]
    weights, outs, full = refs[:4], refs[4:-1], refs[-1]
    mine = pl.ds(pl.multiple_of(core * TOK, TOK), TOK)
    other = pl.ds(pl.multiple_of((1 - core) * TOK, TOK), TOK)
    for source, whose in ((ours, core), (theirs, 1 - core)):
        lanes = pl.ds(pl.multiple_of(whose * HALF, HALF), HALF)
        full[0:TOK, lanes] = source[mine, :]
        full[TOK:, lanes] = source[other, :]
    total = 0.0
    for weight, dy in zip(weights, (0, -1, 1, 2)):
        deep = weight.shape[0]
        start = lax.rem(row + dy + rows_of, rows_of) * deep
        left = full[:, pl.ds(pl.multiple_of(start, 128), deep)]
        total = total + jnp.dot(left, weight[...], preferred_element_type=F32)
    each = TOK // len(outs)
    for k, out in enumerate(outs):
        for low in range(2):
            out[low * each : (low + 1) * each] = total[low * TOK + k * each : low * TOK + (k + 1) * each].astype(BF16)


def whole_block(shape):
    return pl.BlockSpec(shape, lambda i, info: (0,) * len(shape))


def core_block(shape):
    return pl.BlockSpec(shape, lambda i, info: (0,) * (len(shape) - 1) + (info[0],))


def call(kernel, name, info, args, in_specs, out_shape, out_specs, scratch=(), grid=1, flops=0, moved=0, vmem=VMEM):
    return pl.pallas_call(
        kernel,
        grid_spec=pltpu.PrefetchScalarGridSpec(
            num_scalar_prefetch=1, grid=(grid,), in_specs=in_specs, out_specs=out_specs, scratch_shapes=scratch
        ),
        out_shape=out_shape,
        compiler_params=pltpu.CompilerParams(vmem_limit_bytes=vmem),
        cost_estimate=pl.CostEstimate(flops=flops, bytes_accessed=moved, transcendentals=0),
        name=name,
    )(info, *args)


def tie(first, *rest):
    return lax.optimization_barrier((first, *rest))


def body(tokens, table, short_kernel, poles, residues, skip, out_weight):
    n_seq, n_tp = lax.axis_size("seq"), lax.axis_size("tp")
    chips = n_seq // 2
    ny = chips // NZ
    vocab, width = table.shape[0], out_weight.shape[1]
    index = lax.axis_index("seq")
    core, chip = index % 2, index // 2
    info = jnp.stack([core, chip, lax.axis_index("tp"), chip // NZ, chip % NZ]).astype(jnp.int32)
    swap = [(i, i ^ 1) for i in range(n_seq)]

    def move_y(value, d):
        return lax.ppermute(value, "seq", [(i, (i + d * 2 * NZ) % n_seq) for i in range(n_seq)])

    def move_z(value, d):
        pairs = [(i, i // (2 * NZ) * 2 * NZ + (i + 2 * d) % (2 * NZ)) for i in range(n_seq)]
        return lax.ppermute(value, "seq", pairs)

    def shifted(value, d):
        return lax.ppermute(value, "seq", [(i, i + 2 * d) for i in range(n_seq - 2 * d)])

    ids = tokens.reshape(1, TOK)
    before = lax.ppermute(ids, "seq", [(2 * p + 1, 2 * p + 2) for p in range(chips - 1)])
    cols = width // 2
    mine = lax.dynamic_slice_in_dim(out_weight, core * cols, cols, axis=1)
    came = lax.ppermute(lax.dynamic_slice_in_dim(out_weight, (1 - core) * cols, cols, axis=1), "seq", swap)
    block = jnp.concatenate([jnp.where(core == 0, mine, came), jnp.where(core == 0, came, mine)], axis=0)
    block, before = tie(block, before)
    other = lax.ppermute(jnp.concatenate([ids, before], axis=0), "seq", swap)
    ring = [block, move_z(block, 1), move_z(block, -1)]

    ids_block = whole_block((1, TOK))
    tok_block = whole_block((2 * TOK, HALF))
    flat_block = whole_block((4 * MODES, 128))
    flat = jax.ShapeDtypeStruct((4 * MODES, 128), F32)
    query, base, states, first = call(
        scan_kernel, "scan", info,
        (ids, other, before, jnp.transpose(table, (1, 0, 2)), short_kernel, poles, residues, skip.reshape(1, -1)),
        [ids_block, whole_block((2, TOK)), ids_block]
        + [core_block((3, vocab, HALF)), core_block((3, 3, HALF)), core_block((MODES, HALF)), core_block((MODES, HALF)), core_block((1, HALF))],
        (jax.ShapeDtypeStruct((2 * TOK, HALF), F32), jax.ShapeDtypeStruct((2 * TOK, HALF), F32), jax.ShapeDtypeStruct((chips, 4 * MODES, 128), BF16), flat),
        (tok_block, tok_block, whole_block((chips, 4 * MODES, 128)), flat_block),
        scratch=(
            pltpu.VMEM((3, 2 * TOK + 16, HALF), F32),
            pltpu.VMEM((8 * STEP, 128), F32),
            pltpu.VMEM((8 * STEP, 128), F32),
            pltpu.VMEM((MODES * 8, 128), F32),
            pltpu.VMEM((MODES * 8, 128), F32),
            pltpu.VMEM((MODES * 8, 128), F32),
        ),
        flops=600_000_000, moved=8_000_000,
    )
    states, *ring = tie(states, *ring)
    for _ in range(2):
        ring += [move_z(ring[-2], 1), move_z(ring[-1], -1)]
    part = cols // 2
    ring += [move_z(ring[-2][:, :part], 1), move_z(ring[-1][:, part:], -1)]
    part_rows = whole_block((32 * NZ, part))
    one, two = call(
        place_kernel, "place", info, ring,
        [whole_block((32, cols))] * 7 + [whole_block((32, part))] * 2,
        (jax.ShapeDtypeStruct((32 * NZ, part), BF16),) * 2,
        (part_rows,) * 2,
        flops=1_000_000, moved=2_000_000, vmem=VMEM // 3,
    )
    states, one, two = tie(states, one, two)
    up, down, down_two = move_y(one, 1), move_y(one, -1), move_y(two, -1)
    states = lax.all_to_all(
        states, "seq", 0, 0, axis_index_groups=[[2 * p + c for p in range(chips)] for c in range(2)]
    )
    two_late, up = tie(two, up)
    across_one = move_y(up, 1)
    up_two = move_y(two_late, 1)
    across_two = move_y(down_two, -1)
    weights = ((one, up, down, across_one), (two, up_two, down_two, across_two))
    gated = call(
        functools.partial(gate_kernel, n_tp), "gate", info, (states, first, poles, residues, query, base),
        [whole_block((chips, 4 * MODES, 128)), flat_block, core_block((MODES, HALF)), core_block((MODES, HALF)), tok_block, tok_block],
        jax.ShapeDtypeStruct((2 * TOK, HALF), BF16),
        tok_block,
        scratch=(
            pltpu.VMEM((MODES * 8, 128), F32),
            pltpu.VMEM((MODES * 8, 128), F32),
            pltpu.VMEM((8 * STEP, 128), F32),
            pltpu.VMEM((2 * TOK, HALF), F32),
        ),
        flops=20_000_000, moved=4_000_000,
    )
    partner = lax.ppermute(gated, "seq", swap)
    rows = TOK // n_tp
    tile = part // 2
    sides = ([], [])
    for group in weights:
        parts = call(
            functools.partial(project_kernel, ny), "project", info, (gated, partner, *group),
            [tok_block, tok_block] + [pl.BlockSpec((w.shape[0], tile), lambda i, info: (0, i)) for w in group],
            (jax.ShapeDtypeStruct((2 * rows, part), BF16),) * n_tp,
            (pl.BlockSpec((2 * rows, tile), lambda i, info: (0, i)),) * n_tp,
            scratch=(pltpu.VMEM((2 * TOK, 2 * HALF), BF16),),
            grid=part // tile, flops=4 * TOK * 2 * HALF * part, moved=2 * HALF * part * 2, vmem=VMEM // 3,
        )
        total = parts[0].astype(F32)
        for d in range(1, n_tp):
            total = total + lax.ppermute(parts[d], "tp", [(x, (x + d) % n_tp) for x in range(n_tp)]).astype(F32)
        total = total.astype(BF16)
        sides[0].append(total[:rows])
        sides[1].append(lax.ppermute(total[rows:], "seq", swap))
    return jnp.where(core == 0, jnp.concatenate(sides[0] + sides[1], axis=1), jnp.concatenate(sides[1] + sides[0], axis=1))


def solution(mesh):
    placed = (
        P("seq"),
        P(None, None, "tp"),
        P(None, None, "tp"),
        P(None, "tp"),
        P(None, "tp"),
        P("tp"),
        P(("tp", "seq"), None),
    )
    return jax.shard_map(
        body, mesh=mesh, in_specs=placed, out_specs=P(("seq", "tp"), None), check_vma=False
    )
```

```python
import functools

import jax
import jax.numpy as jnp
from jax import lax
from jax.experimental import pallas as pl
from jax.experimental.pallas import tpu as pltpu
from jax.sharding import PartitionSpec as P

F32 = jnp.float32
BF16 = jnp.bfloat16
TOK = 128
HALF = 512
MODES = 16
STEP = 136
VMEM = 62 * 1024 * 1024
NZ = 8
ALONG = (0, -1, 1, -2, 2, -3, 3)


def segment_rows(t):
    return pl.ds(t, 8, stride=STEP)


def spread(scratch, value, first):
    for q in range(4):
        scratch[pl.ds(first + q, MODES, stride=8), :] = value[:, q * 128 : (q + 1) * 128]


def squared(value, times):
    for _ in range(times):
        value = value * value
    return value


def scan_kernel(
    info, own, other, before_near, before_far, table, taps, poles, residues, skip,
    query_out, base_out, states_out, first_out,
    streams, drive_scr, filt_scr, pole_scr, res_scr, state_scr,
):
    core, chip = info[0], info[1]
    ids_own, ids_other = own[...], other[...]
    first = jnp.where(core == 0, ids_own, ids_other)
    second = jnp.where(core == 0, ids_other, ids_own)
    before = jnp.where(chip == 0, -1, jnp.where(core == 0, before_near[...], before_far[...]))
    hots = []
    for ids, low in ((before, TOK - 16), (first, 0), (second, 0)):
        column = jnp.transpose(jnp.broadcast_to(ids, (128, TOK)))[low:]
        parts = [
            (column == lax.broadcasted_iota(jnp.int32, column.shape, 1) + 128 * k).astype(F32)
            for k in range(4)
        ]
        hots.append(jnp.concatenate(parts, axis=1))
    hot = jnp.concatenate(hots, axis=0).astype(BF16)
    for j in range(3):
        streams[j] = jnp.dot(hot, table[j], preferred_element_type=F32)

    def mixed(j):
        return (
            taps[0, j : j + 1] * streams[j, 16 : 16 + 2 * TOK]
            + taps[1, j : j + 1] * streams[j, 15 : 15 + 2 * TOK]
            + taps[2, j : j + 1] * streams[j, 14 : 14 + 2 * TOK]
        )

    drive = mixed(1) * mixed(2)
    for s in range(2):
        for q in range(4):
            row = (s * 4 + q) * STEP
            drive_scr[row : row + TOK] = drive[s * TOK : (s + 1) * TOK, q * 128 : (q + 1) * 128]
    for first_row in (0, 4):
        spread(pole_scr, poles[...], first_row)
        spread(res_scr, residues[...], first_row)
    pole = [pole_scr[n * 8 : (n + 1) * 8] for n in range(MODES)]
    res = [res_scr[n * 8 : (n + 1) * 8] for n in range(MODES)]

    def advance(t, modes):
        value = drive_scr[segment_rows(t), :]
        modes = tuple(pole[n] * modes[n] + value for n in range(MODES))
        terms = [res[n] * modes[n] for n in range(MODES)]
        while len(terms) > 1:
            terms = [a + b for a, b in zip(terms[::2], terms[1::2])]
        filt_scr[segment_rows(t), :] = terms[0]
        return modes

    modes = lax.fori_loop(0, TOK, advance, (jnp.zeros((8, 128), F32),) * MODES, unroll=4)
    for n in range(MODES):
        state_scr[n * 8 : (n + 1) * 8] = modes[n]
    query = mixed(0)
    query_out[...] = query
    ends = []
    for q in range(4):
        lanes = slice(q * 128, (q + 1) * 128)
        rows = slice(q * MODES, (q + 1) * MODES)
        one = state_scr[pl.ds(q, MODES, stride=8), :]
        two = state_scr[pl.ds(4 + q, MODES, stride=8), :]
        half = squared(poles[:, lanes], 7)
        first_out[rows] = one
        ends.append((half * one + two).astype(BF16))
        for s in range(2):
            rows = slice(s * TOK, (s + 1) * TOK)
            row = (s * 4 + q) * STEP
            filtered = filt_scr[row : row + TOK] + skip[:, lanes] * drive[rows, lanes]
            base_out[rows, lanes] = query[rows, lanes] * filtered
    end = jnp.concatenate(ends, axis=0)
    for chip_to in range(states_out.shape[0]):
        states_out[chip_to] = end


def gate_kernel(
    groups, info, states, first, poles, residues, query, base, gated_out, coef_scr, pole_scr, corr_scr, gated_scr
):
    place, each = info[2], TOK // groups
    pole = jnp.concatenate([poles[:, q * 128 : (q + 1) * 128] for q in range(4)], axis=0)
    lead = jnp.concatenate([residues[:, q * 128 : (q + 1) * 128] for q in range(4)], axis=0) * pole
    half = squared(pole, 7)
    whole = half * half

    def join(source, running):
        return whole * running + states[source].astype(F32)

    incoming = lax.fori_loop(0, info[1], join, jnp.zeros((4 * MODES, 128), F32))
    coefs = (lead * incoming, lead * (half * incoming + first[...]))
    for s in range(2):
        for q in range(4):
            coef_scr[pl.ds(s * 4 + q, MODES, stride=8), :] = coefs[s][q * MODES : (q + 1) * MODES]
        spread(pole_scr, poles[...], s * 4)
    mode_pole = [pole_scr[n * 8 : (n + 1) * 8] for n in range(MODES)]
    start = tuple(coef_scr[n * 8 : (n + 1) * 8] for n in range(MODES))

    def decay(t, terms):
        total = list(terms)
        while len(total) > 1:
            total = [a + b for a, b in zip(total[::2], total[1::2])]
        corr_scr[segment_rows(t), :] = total[0]
        return tuple(mode_pole[n] * terms[n] for n in range(MODES))

    lax.fori_loop(0, TOK, decay, start, unroll=4)
    for s in range(2):
        for q in range(4):
            rows, lanes = slice(s * TOK, (s + 1) * TOK), slice(q * 128, (q + 1) * 128)
            row = (s * 4 + q) * STEP
            gated_scr[rows, lanes] = base[rows, lanes] + query[rows, lanes] * corr_scr[row : row + TOK]
    for owner in range(2):
        for d in range(groups):
            spot = pl.ds(pl.multiple_of(owner * TOK + lax.rem(place + d, groups) * each, each), each)
            row = owner * TOK + d * each
            gated_out[row : row + each] = gated_scr[spot, :].astype(BF16)


def place_kernel(info, *refs):
    column, blocks, last, outs = info[4], refs[:7], refs[7:9], refs[9:]
    for block, dz in zip(blocks, ALONG):
        rows = pl.ds(pl.multiple_of(lax.rem(column + dz + NZ, NZ) * 32, 32), 32)
        for k, out in enumerate(outs):
            cols = out.shape[1]
            out[rows, :] = block[:, k * cols : (k + 1) * cols]
    rows = pl.ds(pl.multiple_of(lax.rem(column + NZ // 2, NZ) * 32, 32), 32)
    for block, out in zip(last, outs):
        out[rows, :] = block[...]


def project_kernel(rows_of, info, ours, theirs, *refs):
    core, row = info[0], info[3]
    weights, outs, full = refs[:4], refs[4:-1], refs[-1]
    mine = pl.ds(pl.multiple_of(core * TOK, TOK), TOK)
    other = pl.ds(pl.multiple_of((1 - core) * TOK, TOK), TOK)
    for source, whose in ((ours, core), (theirs, 1 - core)):
        lanes = pl.ds(pl.multiple_of(whose * HALF, HALF), HALF)
        full[0:TOK, lanes] = source[mine, :]
        full[TOK:, lanes] = source[other, :]
    total = 0.0
    for weight, dy in zip(weights, (0, -1, 1, 2)):
        deep = weight.shape[0]
        start = lax.rem(row + dy + rows_of, rows_of) * deep
        left = full[:, pl.ds(pl.multiple_of(start, 128), deep)]
        total = total + jnp.dot(left, weight[...], preferred_element_type=F32)
    each = TOK // len(outs)
    for k, out in enumerate(outs):
        for low in range(2):
            out[low * each : (low + 1) * each] = total[low * TOK + k * each : low * TOK + (k + 1) * each].astype(BF16)


def whole_block(shape):
    return pl.BlockSpec(shape, lambda i, info: (0,) * len(shape))


def core_block(shape):
    return pl.BlockSpec(shape, lambda i, info: (0,) * (len(shape) - 1) + (info[0],))


def call(kernel, name, info, args, in_specs, out_shape, out_specs, scratch=(), grid=1, flops=0, moved=0, vmem=VMEM):
    return pl.pallas_call(
        kernel,
        grid_spec=pltpu.PrefetchScalarGridSpec(
            num_scalar_prefetch=1, grid=(grid,), in_specs=in_specs, out_specs=out_specs, scratch_shapes=scratch
        ),
        out_shape=out_shape,
        compiler_params=pltpu.CompilerParams(vmem_limit_bytes=vmem),
        cost_estimate=pl.CostEstimate(flops=flops, bytes_accessed=moved, transcendentals=0),
        name=name,
    )(info, *args)


def tie(first, *rest):
    return lax.optimization_barrier((first, *rest))


def body(tokens, table, short_kernel, poles, residues, skip, out_weight):
    n_seq, n_tp = lax.axis_size("seq"), lax.axis_size("tp")
    chips = n_seq // 2
    ny = chips // NZ
    vocab, width = table.shape[0], out_weight.shape[1]
    index = lax.axis_index("seq")
    core, chip = index % 2, index // 2
    info = jnp.stack([core, chip, lax.axis_index("tp"), chip // NZ, chip % NZ]).astype(jnp.int32)
    swap = [(i, i ^ 1) for i in range(n_seq)]

    def move_y(value, d):
        return lax.ppermute(value, "seq", [(i, (i + d * 2 * NZ) % n_seq) for i in range(n_seq)])

    def move_z(value, d):
        pairs = [(i, i // (2 * NZ) * 2 * NZ + (i + 2 * d) % (2 * NZ)) for i in range(n_seq)]
        return lax.ppermute(value, "seq", pairs)

    def shifted(value, d):
        return lax.ppermute(value, "seq", [(i, i + 2 * d) for i in range(n_seq - 2 * d)])

    ids = tokens.reshape(1, TOK)
    before = lax.ppermute(ids, "seq", [(2 * p + 1, 2 * p + 2) for p in range(chips - 1)])
    cols = width // 2
    mine = lax.dynamic_slice_in_dim(out_weight, core * cols, cols, axis=1)
    came = lax.ppermute(lax.dynamic_slice_in_dim(out_weight, (1 - core) * cols, cols, axis=1), "seq", swap)
    block = jnp.concatenate([jnp.where(core == 0, mine, came), jnp.where(core == 0, came, mine)], axis=0)
    block, before = tie(block, before)
    other, passed = lax.ppermute(ids, "seq", swap), lax.ppermute(before, "seq", swap)
    ring = [block, move_z(block, 1), move_z(block, -1)]

    ids_block = whole_block((1, TOK))
    tok_block = whole_block((2 * TOK, HALF))
    flat_block = whole_block((4 * MODES, 128))
    flat = jax.ShapeDtypeStruct((4 * MODES, 128), F32)
    query, base, states, first = call(
        scan_kernel, "scan", info,
        (ids, other, before, passed, jnp.transpose(table, (1, 0, 2)), short_kernel, poles, residues, skip.reshape(1, -1)),
        [ids_block] * 4
        + [core_block((3, vocab, HALF)), core_block((3, 3, HALF)), core_block((MODES, HALF)), core_block((MODES, HALF)), core_block((1, HALF))],
        (jax.ShapeDtypeStruct((2 * TOK, HALF), F32), jax.ShapeDtypeStruct((2 * TOK, HALF), F32), jax.ShapeDtypeStruct((chips, 4 * MODES, 128), BF16), flat),
        (tok_block, tok_block, whole_block((chips, 4 * MODES, 128)), flat_block),
        scratch=(
            pltpu.VMEM((3, 2 * TOK + 16, HALF), F32),
            pltpu.VMEM((8 * STEP, 128), F32),
            pltpu.VMEM((8 * STEP, 128), F32),
            pltpu.VMEM((MODES * 8, 128), F32),
            pltpu.VMEM((MODES * 8, 128), F32),
            pltpu.VMEM((MODES * 8, 128), F32),
        ),
        flops=600_000_000, moved=8_000_000,
    )
    states, *ring = tie(states, *ring)
    for _ in range(2):
        ring += [move_z(ring[-2], 1), move_z(ring[-1], -1)]
    part = cols // 2
    ring += [move_z(ring[-2][:, :part], 1), move_z(ring[-1][:, part:], -1)]
    part_rows = whole_block((32 * NZ, part))
    one, two = call(
        place_kernel, "place", info, ring,
        [whole_block((32, cols))] * 7 + [whole_block((32, part))] * 2,
        (jax.ShapeDtypeStruct((32 * NZ, part), BF16),) * 2,
        (part_rows,) * 2,
        flops=1_000_000, moved=2_000_000, vmem=VMEM // 3,
    )
    states, one, two = tie(states, one, two)
    up, down, down_two = move_y(one, 1), move_y(one, -1), move_y(two, -1)
    states = lax.all_to_all(
        states, "seq", 0, 0, axis_index_groups=[[2 * p + c for p in range(chips)] for c in range(2)]
    )
    two_late, up = tie(two, up)
    across_one = move_y(up, 1)
    up_two = move_y(two_late, 1)
    across_two = move_y(down_two, -1)
    weights = ((one, up, down, across_one), (two, up_two, down_two, across_two))
    gated = call(
        functools.partial(gate_kernel, n_tp), "gate", info, (states, first, poles, residues, query, base),
        [whole_block((chips, 4 * MODES, 128)), flat_block, core_block((MODES, HALF)), core_block((MODES, HALF)), tok_block, tok_block],
        jax.ShapeDtypeStruct((2 * TOK, HALF), BF16),
        tok_block,
        scratch=(
            pltpu.VMEM((MODES * 8, 128), F32),
            pltpu.VMEM((MODES * 8, 128), F32),
            pltpu.VMEM((8 * STEP, 128), F32),
            pltpu.VMEM((2 * TOK, HALF), F32),
        ),
        flops=20_000_000, moved=4_000_000,
    )
    partner = lax.ppermute(gated, "seq", swap)
    rows = TOK // n_tp
    tile = part // 2
    sides = []
    for group in weights:
        parts = call(
            functools.partial(project_kernel, ny), "project", info, (gated, partner, *group),
            [tok_block, tok_block] + [pl.BlockSpec((w.shape[0], tile), lambda i, info: (0, i)) for w in group],
            (jax.ShapeDtypeStruct((2 * rows, part), BF16),) * n_tp,
            (pl.BlockSpec((2 * rows, tile), lambda i, info: (0, i)),) * n_tp,
            scratch=(pltpu.VMEM((2 * TOK, 2 * HALF), BF16),),
            grid=part // tile, flops=4 * TOK * 2 * HALF * part, moved=2 * HALF * part * 2, vmem=VMEM // 3,
        )
        total = parts[0].astype(F32)
        for d in range(1, n_tp):
            total = total + lax.ppermute(parts[d], "tp", [(x, (x + d) % n_tp) for x in range(n_tp)]).astype(F32)
        sides.append(total.astype(BF16))
    near = jnp.concatenate([total[:rows] for total in sides], axis=1)
    far = lax.ppermute(jnp.concatenate([total[rows:] for total in sides], axis=1), "seq", swap)
    return jnp.where(core == 0, jnp.concatenate([near, far], axis=1), jnp.concatenate([far, near], axis=1))


def solution(mesh):
    placed = (
        P("seq"),
        P(None, None, "tp"),
        P(None, None, "tp"),
        P(None, "tp"),
        P(None, "tp"),
        P("tp"),
        P(("tp", "seq"), None),
    )
    return jax.shard_map(
        body, mesh=mesh, in_specs=placed, out_specs=P(("seq", "tp"), None), check_vma=False
    )
```
